32 devices in a mesh: groups: 2 (over x), row: 16 (over z, y, core).
Axes of the slice: x: 2, y: 2, z: 4, core: 2. Of those that a mesh axis runs over, the one named last changes fastest.
Arguments:
- amps: bfloat16 [32, 2, 64, 4096], P(('groups', 'row')), parts along dimension 0, may hold values from -6 to 6
- integrals: bfloat16 [6, 4096, 16384], P('groups', None, 'row'), parts along dimension 0, may hold values from -0.0625 to 0.0625
- domain_mask: int32 [32, 3], P('groups'), parts along dimension 0, may hold values 0 or 1
- tile_list: int32 [32, 2], P('groups'), parts along dimension 0, may hold values from 0 to 2, as said below
- mirror: int32 [32], P('groups'), parts along dimension 0, may hold values from 0 to 15, as said below
Outputs:
- residual: bfloat16 [32, 64, 16384], P('groups', None, 'row'), parts along dimension 0
The draws below stay inside these ranges and needn't reach their ends.
There are 2 independent parts, one for each index of `groups`. The reference program is written for one: setup_inputs(seed, part) draws one part's arguments, and reference() takes and returns one part's arrays. A program takes and returns all parts, laid end to end along the dimension named above; each array names one. Nothing has to cross between parts.
Inputs may be any that keep to these rules, and one draw needn't show every extreme that they name: `tile_list`: each row names 2 different virtual-pair tiles. mirror[mirror[p]] = p and mirror[p] != p for every p.
All inputs are finite; a program needn't handle non-finite values.
Results may differ from the reference program's by a relative error of at most 0.001.
Values may be sent and summed in bfloat16 or wider, within the bound.
No kernel may reach another device: no remote copies, remote signals or barrier semaphores. Data moves between devices by JAX's collectives and lax.ppermute only.
A program may use at most 192 MiB of HBM per device.

```python
import jax
import jax.numpy as jnp

VT = 64
OT = 8
WT = 2
CT = 3
KT = 2
PW = 64
CD = 4096
AB = 16384
PTILES = 16


def draw_tile_list(key, part):
    key = jax.random.fold_in(key, 11)
    row_keys = jax.random.split(key, PTILES)

    def one_row(row_key):
        return jax.random.permutation(row_key, CT)[:KT]
    return jax.vmap(one_row)(row_keys).astype(jnp.int32)


def draw_mirror(key, part):
    key = jax.random.fold_in(key, 12)
    shuffled = jax.random.permutation(key, PTILES).astype(jnp.int32)
    halfway = PTILES // 2
    first_half = shuffled[:halfway]
    second_half = shuffled[halfway:]
    result = jnp.zeros((PTILES,), jnp.int32)
    result = result.at[first_half].set(second_half)
    result = result.at[second_half].set(first_half)
    return result


def with_ends(entries, stream_key, low, largest):
    spot = [jax.random.randint(jax.random.fold_in(stream_key, axis), (), 0, length) for axis, length in enumerate(entries.shape)]
    main_axis = entries.shape.index(max(entries.shape))
    neighbour = spot[:main_axis] + [(spot[main_axis] + 1) % entries.shape[main_axis]] + spot[main_axis + 1:]
    return entries.at[tuple(spot)].set(low).at[tuple(neighbour)].set(largest)


def block_scale(own_key, extent, pieces, least, largest):
    def one(axis_at, blocks):
        heights = jax.random.uniform(jax.random.fold_in(jax.random.fold_in(own_key, 6), axis_at), (blocks,), jnp.float32, least / len(pieces), largest / len(pieces))
        return jnp.repeat(jnp.exp(heights), extent[axis_at] // blocks).reshape((-1,) + (1,) * (len(extent) - axis_at - 1))

    loudness = one(*pieces[0])
    for cut in pieces[1:]:
        loudness = loudness * one(*cut)
    return loudness


def bell_draw(own_key, dims, scale, reach, shards=(), held_as=jnp.bfloat16):
    level = block_scale(own_key, dims, shards, -0.22, 0.18) if shards else 1.0
    array = jax.random.normal(own_key, dims, jnp.float32) * scale * level
    return jnp.minimum(jnp.maximum(array, -reach), reach).astype(held_as)


def setup_inputs(seed: int = 0, part: int = 0) -> dict:
    key_list = jax.random.split(jax.random.key(seed), 6)
    own_keys = jax.random.split(jax.random.fold_in(key_list[5], part), 6)
    return {
        "amps": bell_draw(own_keys[0], (PTILES, KT, PW, CD), 1.0, 6.0, ((0, 16),)),
        "integrals": bell_draw(own_keys[1], (CT, CD, AB), (KT * CD) ** -0.5, 0.0625, ((2, 16),)),
        "domain_mask": with_ends((jax.random.randint(own_keys[2], (PTILES, CT), 0, 4) < 3).astype(jnp.int32), jax.random.fold_in(own_keys[2], 1), 0, 1),
        "tile_list": draw_tile_list(jax.random.fold_in(jax.random.fold_in(key_list[5], part), 71), part),
        "mirror": draw_mirror(jax.random.fold_in(jax.random.fold_in(key_list[5], part), 71), part),
    }


def reference(amps, integrals, domain_mask, tile_list, mirror):
    alive_slots = jnp.take_along_axis(domain_mask, tile_list, axis=1)
    row_count = PTILES * PW
    direct = jnp.zeros((row_count, AB), jnp.float32)
    for cd_tile in range(CT):
        weights = (alive_slots * (tile_list == cd_tile)).astype(jnp.float32)
        merged = jnp.einsum("pk,pkqd->pqd", weights, amps.astype(jnp.float32))
        merged = merged.astype(jnp.bfloat16).reshape(row_count, CD)
        direct = direct + jnp.dot(merged, integrals[cd_tile], preferred_element_type=jnp.float32)
    span_width = VT * WT
    reshaped = direct.reshape(PTILES, OT, OT, span_width, span_width)
    mirrored = jnp.transpose(reshaped[mirror], (0, 2, 1, 4, 3)).reshape(PTILES, PW, AB)
    return (direct.reshape(PTILES, PW, AB) + mirrored).astype(jnp.bfloat16)
```

```python
import functools
import math

import jax
import jax.numpy as jnp
from jax import lax
from jax.experimental import pallas as pl
from jax.experimental.pallas import tpu as pltpu
from jax.sharding import PartitionSpec as P

OT = 8
LEVELS = 32767.0
STEPS_PER_OCTAVE = 64.0
CODE_ROWS = 16
VMEM_LIMIT = 56 * 1024 * 1024


def ring_order(mesh):
    size = mesh.shape["row"] // 2
    chips = [getattr(d, "coords", (0, 0, n)) for n, d in enumerate(mesh.devices[0, ::2])]
    columns = sorted({c[1] for c in chips})
    order = sorted(range(size), key=lambda n: (chips[n][1], chips[n][2]))
    if len(columns) == 2:
        half = size // 2
        order = order[:half] + order[half:][::-1]
    return order


def ladder_kernel(slots, first, pair_rows, meta, wcode, *refs):
    blocks = refs[: 4 * slots]
    refs = refs[4 * slots :]
    integrals = refs[0]
    refs = refs[1 if first else 2 :]
    direct, message, codes, lhs, acc, turned, sem = refs
    step = pl.program_id(0)
    tiles = integrals.shape[0]
    core = meta[0]

    @pl.when(step == 0)
    def _():
        acc[...] = jnp.zeros_like(acc)

    for t in range(tiles):
        for u in range(slots):
            for c in range(2):
                own_core = core if c == 0 else 1 - core
                p = meta[1 + u] * 2 + own_core
                code = wcode[p * tiles + t]
                a0, a1 = blocks[4 * u + 2 * c], blocks[4 * u + 2 * c + 1]
                row = pl.multiple_of(u * 2 * pair_rows + own_core * pair_rows, pair_rows)
                rows = pl.ds(row, pair_rows)

                @pl.when(code == 0)
                def _():
                    lhs[t, rows, :] = jnp.zeros((pair_rows, lhs.shape[2]), lhs.dtype)

                @pl.when(code == 1)
                def _():
                    lhs[t, rows, :] = a0[...]

                @pl.when(code == 2)
                def _():
                    lhs[t, rows, :] = a1[...]

    total = acc[...]
    for t in range(tiles):
        total += jnp.dot(lhs[t], integrals[t], preferred_element_type=jnp.float32)
    acc[...] = total

    @pl.when(step == pl.num_programs(0) - 1)
    def _():
        copies = []
        height = 2 * pair_rows
        for u in range(slots):
            start = pl.multiple_of(meta[1 + u] * height, height)
            copies.append(
                pltpu.make_async_copy(
                    acc.at[pl.ds(u * height, height), :], direct.at[pl.ds(start, height), :], sem.at[u]
                )
            )
            copies[-1].start()
        for u in range(slots):
            local_rows = acc.shape[1] // 128
            for a in range(local_rows):
                piece = acc[u * height : (u + 1) * height, a * 128 : (a + 1) * 128]
                turned[pl.ds(a, 128, stride=local_rows), :] = piece.T
            values = turned[...]
            largest = jnp.max(jnp.abs(values), axis=0, keepdims=True)
            code = jnp.ceil(jnp.log2(jnp.maximum(largest, 1e-30)) * STEPS_PER_OCTAVE) + 1.0
            scale = jnp.exp2(code * (-1.0 / STEPS_PER_OCTAVE)) * LEVELS
            whole = jnp.round(values * scale).astype(jnp.int32).astype(jnp.int16)
            depth = message.shape[1] // slots
            message[:, u * depth : (u + 1) * depth, :] = whole.reshape(message.shape[0], depth, height)
            codes[u : u + 1, :] = code.astype(jnp.int32)
        for copy in copies:
            copy.wait()


def ladder(meta, wcode, blocks, integrals, direct, number):
    slots = len(blocks) // 4
    pair_rows, cd_width = blocks[0].shape
    tiles, _, columns = integrals.shape
    first = direct is None
    local_rows = columns // 128
    depth = 128 // number * local_rows
    chunk = 512
    height = 2 * pair_rows
    in_specs = [pl.BlockSpec((pair_rows, chunk), lambda k, *_: (0, k)) for _ in blocks]
    in_specs.append(pl.BlockSpec((tiles, chunk, columns), lambda k, *_: (0, k, 0)))
    operands = [meta, wcode, *blocks, integrals]
    aliases = {}
    if not first:
        in_specs.append(pl.BlockSpec(memory_space=pl.ANY))
        aliases = {len(operands): 0}
        operands.append(direct)
    flops = 2 * slots * height * tiles * cd_width * columns
    return pl.pallas_call(
        functools.partial(ladder_kernel, slots, first, pair_rows),
        grid_spec=pltpu.PrefetchScalarGridSpec(
            num_scalar_prefetch=2,
            grid=(cd_width // chunk,),
            in_specs=in_specs,
            out_specs=[
                pl.BlockSpec(memory_space=pl.ANY),
                pl.BlockSpec((number, slots * depth, height), lambda k, *_: (0, 0, 0)),
                pl.BlockSpec((slots, height), lambda k, *_: (0, 0)),
            ],
            scratch_shapes=[
                pltpu.VMEM((tiles, slots * height, chunk), jnp.bfloat16),
                pltpu.VMEM((slots * height, columns), jnp.float32),
                pltpu.VMEM((columns, height), jnp.float32),
                pltpu.SemaphoreType.DMA((slots,)),
            ],
        ),
        out_shape=[
            jax.ShapeDtypeStruct((number * pair_rows, columns), jnp.float32),
            jax.ShapeDtypeStruct((number, slots * depth, height), jnp.int16),
            jax.ShapeDtypeStruct((slots, height), jnp.int32),
        ],
        input_output_aliases=aliases,
        compiler_params=pltpu.CompilerParams(vmem_limit_bytes=VMEM_LIMIT),
        cost_estimate=pl.CostEstimate(flops=flops, bytes_accessed=integrals.size * 2, transcendentals=0),
        name=f"ladder{slots}",
    )(*operands)


def symmetrize_kernel(places, local_rows, pair_rows, mirror, codes, *refs):
    received = refs[: len(refs) - 7]
    direct, residual, own, rounded, turned, in_sem, out_sem = refs[len(refs) - 7 :]
    number, columns = own.shape[0], own.shape[2]
    chips = number // 2
    height = 2 * pair_rows
    depth = local_rows * local_rows
    loads, stores = [], []
    for m in range(number):
        p = mirror[m]
        loads.append(pltpu.make_async_copy(direct.at[p], own.at[m], in_sem.at[m]))
        stores.append(pltpu.make_async_copy(rounded.at[m], residual.at[p], out_sem.at[m]))
        loads[m].start()
    row = lax.broadcasted_iota(jnp.int32, (height, height), 0)
    lane = lax.broadcasted_iota(jnp.int32, (height, height), 1)
    inner = row % pair_rows
    partner = row - inner + (inner % OT) * OT + inner // OT
    pick = jnp.where(lane == partner, 1.0, 0.0).astype(jnp.bfloat16)
    pick = jnp.concatenate([pick, pick], axis=1)
    for chip in range(chips):
        for i in range(number):
            which, u, place = places(chip, i // 2)
            whole = received[which][i, u * depth : (u + 1) * depth, :].astype(jnp.int32).astype(jnp.float32)
            code = codes[i, place : place + 1, :].astype(jnp.float32)
            scale = jnp.exp2(code * (1.0 / STEPS_PER_OCTAVE)) * (1.0 / LEVELS)
            whole = whole * scale
            for b in range(local_rows):
                at = (b * number + i) * local_rows
                turned[at : at + local_rows, :] = whole[b * local_rows : (b + 1) * local_rows, :]
        values = turned[...]
        high = values.astype(jnp.bfloat16)
        low = (values - high.astype(jnp.float32)).astype(jnp.bfloat16)
        both = jnp.concatenate([high, low], axis=1)
        mirrored = lax.dot_general(pick, both, (((1,), (1,)), ((), ())), preferred_element_type=jnp.float32)
        for h in range(2):
            m = chip * 2 + h
            loads[m].wait()
            rounded[m] = (own[m] + mirrored[h * pair_rows : (h + 1) * pair_rows, :]).astype(jnp.bfloat16)
            stores[m].start()
    for m in range(number):
        stores[m].wait()


def symmetrize(mirror, codes, received, direct, places):
    number, pair_rows, columns = direct.shape
    local_rows = columns // 128
    height = 2 * pair_rows
    return pl.pallas_call(
        functools.partial(symmetrize_kernel, places, local_rows, pair_rows),
        in_specs=[
            pl.BlockSpec(memory_space=pltpu.SMEM),
            pl.BlockSpec(memory_space=pltpu.VMEM),
            *[pl.BlockSpec(memory_space=pltpu.VMEM) for _ in received],
            pl.BlockSpec(memory_space=pl.ANY),
        ],
        out_specs=pl.BlockSpec(memory_space=pl.ANY),
        out_shape=jax.ShapeDtypeStruct(direct.shape, jnp.bfloat16),
        scratch_shapes=[
            pltpu.VMEM(direct.shape, jnp.float32),
            pltpu.VMEM(direct.shape, jnp.bfloat16),
            pltpu.VMEM((columns, height), jnp.float32),
            pltpu.SemaphoreType.DMA((number,)),
            pltpu.SemaphoreType.DMA((number,)),
        ],
        compiler_params=pltpu.CompilerParams(vmem_limit_bytes=VMEM_LIMIT),
        cost_estimate=pl.CostEstimate(flops=0, bytes_accessed=direct.size * 8, transcendentals=0),
        name="symmetrize",
    )(mirror, codes, *received, direct)


def local(order, amps, integrals, domain_mask, tile_list, mirror):
    number = mirror.shape[0]
    pair_rows, cd_width = amps.shape[2:]
    tiles = integrals.shape[0]
    chips = len(order)
    half = chips // 2
    position = [order.index(c) for c in range(chips)]
    me = lax.axis_index("row")
    my_position = jnp.array(position, jnp.int32)[me // 2]
    chip_at = jnp.array(order, jnp.int32)
    core = me % 2

    alive = jnp.take_along_axis(domain_mask, tile_list, axis=1)
    which = jnp.arange(tiles, dtype=jnp.int32)
    hits = (tile_list[:, :, None] == which) * alive[:, :, None]
    wcode = jnp.sum(hits * jnp.arange(1, 3, dtype=jnp.int32)[None, :, None], axis=1).reshape(-1)

    def turn(d):
        return [(order[i] * 2 + c, order[(i + d) % chips] * 2 + c) for i in range(chips) for c in range(2)]

    def shift(x, d):
        return lax.ppermute(x, "row", turn(d))

    def twin(x):
        return lax.ppermute(x, "row", [(i, i ^ 1) for i in range(number)])

    def meta(*offsets):
        return jnp.stack([core] + [chip_at[(my_position + o) % chips] for o in offsets])

    mine = [amps[0, 0], amps[0, 1]]
    left, right = list(mine), list(mine)
    direct, messages, codes = None, [], []

    def run(offsets, arrivals):
        nonlocal direct
        blocks = []
        for a in arrivals:
            blocks += [*a, *[twin(x) for x in a]]
        direct, message, code = ladder(meta(*offsets), wcode, blocks, integrals, direct, number)
        messages.append(message)
        codes.append(code)

    where = {0: (0, 0)}
    run([0], [mine])
    for s in range(1, half):
        left = [shift(x, 1) for x in left]
        right = [shift(x, -1) for x in right]
        where[chips - s] = (s, 0)
        where[s] = (s, 1)
        run([-s, s], [left, right])
    where[half] = (half, 0)
    run([half], [[shift(left[0], 1), shift(right[1], -1)]])

    received = [
        lax.all_to_all(m, "row", split_axis=0, concat_axis=0, tiled=True) for m in messages
    ]
    all_codes = jnp.concatenate(codes, axis=0)
    all_codes = lax.all_gather(all_codes, "row", axis=0, tiled=False)

    def places(chip, source):
        s, u = where[(position[chip] - position[source]) % chips]
        return s, u, (0 if s == 0 else 2 * s - 1) + u

    direct = direct.reshape(number, pair_rows, integrals.shape[2])
    return symmetrize(mirror, all_codes, received, direct, places)


def solution(mesh):
    return jax.shard_map(
        functools.partial(local, ring_order(mesh)),
        mesh=mesh,
        in_specs=(
            P(("groups", "row"), None, None, None),
            P("groups", None, "row"),
            P("groups", None),
            P("groups", None),
            P("groups"),
        ),
        out_specs=P("groups", None, "row"),
        check_vma=False,
    )
```

```python
import functools

import jax
import jax.numpy as jnp
from jax import lax
from jax.experimental import pallas as pl
from jax.experimental.pallas import tpu as pltpu
from jax.sharding import PartitionSpec as P

OT = 8
LEVELS = 32767.0
STEPS_PER_OCTAVE = 64.0
CODE_ROWS = 16
SPAN = 128
LADDER_VMEM = 16 * 1024 * 1024
SYMMETRIZE_VMEM = 24 * 1024 * 1024


def ring_order(mesh):
    size = mesh.shape["row"] // 2
    chips = [getattr(d, "coords", (0, 0, n)) for n, d in enumerate(mesh.devices[0, ::2])]
    columns = sorted({c[1] for c in chips})
    order = sorted(range(size), key=lambda n: (chips[n][1], chips[n][2]))
    if len(columns) == 2:
        half = size // 2
        order = order[:half] + order[half:][::-1]
    return order


def hbm(x):
    return pltpu.with_memory_space_constraint(x, pltpu.HBM)


def load_kernel(meta, wcode, source, target, sem):
    copies = [pltpu.make_async_copy(source.at[t], target.at[t], sem.at[t]) for t in range(source.shape[0])]
    for copy in copies:
        copy.start()
    for copy in copies:
        copy.wait()


def load(meta, wcode, integrals):
    return pl.pallas_call(
        load_kernel,
        in_specs=[
            pl.BlockSpec(memory_space=pltpu.SMEM),
            pl.BlockSpec(memory_space=pltpu.SMEM),
            pl.BlockSpec(memory_space=pl.ANY),
        ],
        out_specs=pl.BlockSpec(memory_space=pltpu.VMEM),
        out_shape=pltpu.VMEM(integrals.shape, integrals.dtype),
        scratch_shapes=[pltpu.SemaphoreType.DMA((integrals.shape[0],))],
        compiler_params=pltpu.CompilerParams(vmem_limit_bytes=4 * 1024 * 1024),
        name="load",
    )(meta, wcode, hbm(integrals))


def ladder_kernel(offsets, start_row, earlier, chained, pair_rows, meta, wcode, *refs):
    slots, last = len(offsets), earlier > 0
    if last:
        blocks, refs = refs[:4], refs[4:]
        views = [[(blocks[0], blocks[1]), (blocks[2], blocks[3])]]
    else:
        blocks, refs = refs[: 2 * slots], refs[2 * slots :]
        views = [[(b.at[0], b.at[1]) for b in blocks[2 * u : 2 * u + 2]] for u in range(slots)]
    integrals, refs = refs[0], refs[1:]
    before, refs = refs[:earlier], refs[earlier:]
    direct, *outs, lhs, acc, turned, coded, sem = refs[chained:]
    step = pl.program_id(0)
    tiles = integrals.shape[0]
    chunk = blocks[0].shape[-1]
    columns = acc.shape[1]
    core = meta[0]
    height = 2 * pair_rows

    @pl.when(step == 0)
    def _():
        acc[...] = jnp.zeros_like(acc)

    for t in range(tiles):
        for u in range(slots):
            for c in range(2):
                own_core = core if c == 0 else 1 - core
                p = meta[1 + offsets[u]] * 2 + own_core
                code = wcode[p * tiles + t]
                a0, a1 = views[u][c]
                rows = pl.ds(pl.multiple_of(u * height + own_core * pair_rows, pair_rows), pair_rows)
                lanes = slice(t * chunk, (t + 1) * chunk)

                @pl.when(code == 0)
                def _():
                    lhs[rows, lanes] = jnp.zeros((pair_rows, chunk), lhs.dtype)

                @pl.when(code == 1)
                def _():
                    lhs[rows, lanes] = a0[...]

                @pl.when(code == 2)
                def _():
                    lhs[rows, lanes] = a1[...]

    part = integrals[:, pl.ds(pl.multiple_of(step * chunk, chunk), chunk), :]
    acc[...] += jnp.dot(lhs[...], part.reshape(tiles * chunk, columns), preferred_element_type=jnp.float32)

    @pl.when(step == pl.num_programs(0) - 1)
    def _():
        copies = []
        for u in range(slots):
            start = pl.multiple_of(meta[1 + offsets[u]] * height, height)
            copies.append(
                pltpu.make_async_copy(
                    acc.at[pl.ds(u * height, height), :], direct.at[pl.ds(start, height), :], sem.at[u]
                )
            )
            copies[-1].start()
        local_rows = columns // SPAN
        number = coded.shape[0]
        depth = columns // number
        for u in range(slots):
            for a in range(local_rows):
                piece = acc[u * height : (u + 1) * height, a * SPAN : (a + 1) * SPAN]
                turned[pl.ds(a, SPAN, stride=local_rows), :] = piece.T
            values = turned[...]
            largest = jnp.max(jnp.abs(values), axis=0, keepdims=True)
            code = jnp.ceil(jnp.log2(jnp.maximum(largest, 1e-30)) * STEPS_PER_OCTAVE) + 1.0
            scale = jnp.exp2(code * (-1.0 / STEPS_PER_OCTAVE)) * LEVELS
            whole = jnp.round(values * scale).astype(jnp.int32).astype(jnp.int16)
            coded[:, u * depth : (u + 1) * depth, :] = whole.reshape(number, depth, height)
            if last:
                rows = [*[r[...] for r in before], code.astype(jnp.int32)]
                spare = coded.shape[1] - depth - sum(r.shape[0] for r in rows)
                if spare:
                    rows.append(jnp.zeros((spare, height), jnp.int32))
                table = jnp.concatenate(rows, axis=0).astype(jnp.int16)
                coded[:, depth:, :] = jnp.broadcast_to(table[None], (number, *table.shape))
            else:
                outs[1][u : u + 1, :] = code.astype(jnp.int32)
        target = outs[0].at[:, pl.ds(start_row, coded.shape[1]), :]
        copies.append(pltpu.make_async_copy(coded, target, sem.at[slots]))
        copies[-1].start()
        for copy in copies:
            copy.wait()


def ladder(offsets, meta, wcode, blocks, integrals, chain, number, start_row, message_rows, earlier=()):
    slots = len(offsets)
    pair_rows, cd_width = blocks[0].shape[-2:]
    tiles, _, columns = integrals.shape
    last = len(earlier) > 0
    depth = columns // number
    chunk = 1024
    height = 2 * pair_rows
    rows = slots * depth
    if last:
        rows += -(-(sum(c.shape[0] for c in earlier) + 1) // CODE_ROWS) * CODE_ROWS
    if last:
        in_specs = [pl.BlockSpec((pair_rows, chunk), lambda k, *_: (0, k)) for _ in blocks]
    else:
        shape = (None, blocks[0].shape[1], pair_rows, chunk)
        in_specs = [pl.BlockSpec(shape, lambda k, *_: (0, 0, 0, k)) for _ in blocks]
    in_specs.append(pl.BlockSpec(memory_space=pltpu.VMEM))
    operands = [meta, wcode, *[hbm(b) for b in blocks], pltpu.with_memory_space_constraint(integrals, pltpu.VMEM)]
    for code in earlier:
        in_specs.append(pl.BlockSpec(memory_space=pltpu.VMEM))
        operands.append(code)
    aliases = {}
    for n, array in enumerate(chain):
        in_specs.append(pl.BlockSpec(memory_space=pl.ANY))
        aliases[len(operands)] = n
        operands.append(hbm(array))
    out_specs = [pl.BlockSpec(memory_space=pl.ANY)] * 2
    out_shape = [
        pltpu.HBM((number * pair_rows, columns), jnp.float32),
        pltpu.HBM((number, message_rows, height), jnp.int16),
    ]
    if not last:
        out_specs.append(pl.BlockSpec((slots, height), lambda k, *_: (0, 0)))
        out_shape.append(jax.ShapeDtypeStruct((slots, height), jnp.int32))
    flops = 2 * slots * height * tiles * cd_width * columns
    return pl.pallas_call(
        functools.partial(ladder_kernel, offsets, start_row, len(earlier), len(chain), pair_rows),
        grid_spec=pltpu.PrefetchScalarGridSpec(
            num_scalar_prefetch=2,
            grid=(cd_width // chunk,),
            in_specs=in_specs,
            out_specs=out_specs,
            scratch_shapes=[
                pltpu.VMEM((slots * height, tiles * chunk), jnp.bfloat16),
                pltpu.VMEM((slots * height, columns), jnp.float32),
                pltpu.VMEM((columns, height), jnp.float32),
                pltpu.VMEM((number, rows, height), jnp.int16),
                pltpu.SemaphoreType.DMA((slots + 1,)),
            ],
        ),
        out_shape=out_shape,
        input_output_aliases=aliases,
        compiler_params=pltpu.CompilerParams(vmem_limit_bytes=LADDER_VMEM),
        cost_estimate=pl.CostEstimate(flops=flops, bytes_accessed=1 << 20, transcendentals=0),
        name=f"ladder{slots}",
    )(*operands)


def symmetrize_kernel(
    places, local_rows, pair_rows, mirror, received, direct, residual, own, rounded, turned, in_sem, out_sem
):
    number, columns = own.shape[0], own.shape[2]
    chips = number // 2
    height = 2 * pair_rows
    depth = local_rows * local_rows
    loads, stores = [], []
    for m in range(number):
        p = mirror[m]
        loads.append(pltpu.make_async_copy(direct.at[p], own.at[m], in_sem.at[m]))
        stores.append(pltpu.make_async_copy(rounded.at[m], residual.at[p], out_sem.at[m]))
        loads[m].start()
    row = lax.broadcasted_iota(jnp.int32, (height, height), 0)
    lane = lax.broadcasted_iota(jnp.int32, (height, height), 1)
    inner = row % pair_rows
    partner = row - inner + (inner % OT) * OT + inner // OT
    pick = jnp.where(lane == partner, 1.0, 0.0).astype(jnp.bfloat16)
    pick = jnp.concatenate([pick, pick], axis=1)
    scales = []
    for i in range(number):
        code = received[i, chips * depth :, :].astype(jnp.int32).astype(jnp.float32)
        scales.append(jnp.exp2(code * (1.0 / STEPS_PER_OCTAVE)) * (1.0 / LEVELS))
    for chip in range(chips):
        for i in range(number):
            place = places(chip, i // 2)
            whole = received[i, place * depth : (place + 1) * depth, :].astype(jnp.int32).astype(jnp.float32)
            whole = whole * scales[i][place : place + 1, :]
            for b in range(local_rows):
                at = (b * number + i) * local_rows
                turned[at : at + local_rows, :] = whole[b * local_rows : (b + 1) * local_rows, :]
        values = turned[...]
        high = values.astype(jnp.bfloat16)
        low = (values - high.astype(jnp.float32)).astype(jnp.bfloat16)
        both = jnp.concatenate([high, low], axis=1)
        mirrored = lax.dot_general(pick, both, (((1,), (1,)), ((), ())), preferred_element_type=jnp.float32)
        for h in range(2):
            m = chip * 2 + h
            loads[m].wait()
            rounded[m] = (own[m] + mirrored[h * pair_rows : (h + 1) * pair_rows, :]).astype(jnp.bfloat16)
            stores[m].start()
    for m in range(number):
        stores[m].wait()


def symmetrize(mirror, received, direct, places):
    number, pair_rows, columns = direct.shape
    local_rows = columns // SPAN
    height = 2 * pair_rows
    return pl.pallas_call(
        functools.partial(symmetrize_kernel, places, local_rows, pair_rows),
        in_specs=[
            pl.BlockSpec(memory_space=pltpu.SMEM),
            pl.BlockSpec(memory_space=pltpu.VMEM),
            pl.BlockSpec(memory_space=pl.ANY),
        ],
        out_specs=pl.BlockSpec(memory_space=pl.ANY),
        out_shape=jax.ShapeDtypeStruct(direct.shape, jnp.bfloat16),
        scratch_shapes=[
            pltpu.VMEM(direct.shape, jnp.float32),
            pltpu.VMEM(direct.shape, jnp.bfloat16),
            pltpu.VMEM((columns, height), jnp.float32),
            pltpu.SemaphoreType.DMA((number,)),
            pltpu.SemaphoreType.DMA((number,)),
        ],
        compiler_params=pltpu.CompilerParams(vmem_limit_bytes=SYMMETRIZE_VMEM),
        cost_estimate=pl.CostEstimate(flops=0, bytes_accessed=direct.size * 8, transcendentals=0),
        name="symmetrize",
    )(mirror, received, hbm(direct))


def local(order, amps, integrals, domain_mask, tile_list, mirror):
    number = mirror.shape[0]
    pair_rows, cd_width = amps.shape[2:]
    tiles = integrals.shape[0]
    chips = len(order)
    half = chips // 2
    position = [order.index(c) for c in range(chips)]
    me = lax.axis_index("row")
    my_position = jnp.array(position, jnp.int32)[me // 2]
    chip_at = jnp.array(order, jnp.int32)
    core = me % 2

    alive = jnp.take_along_axis(domain_mask, tile_list, axis=1)
    which = jnp.arange(tiles, dtype=jnp.int32)
    hits = (tile_list[:, :, None] == which) * alive[:, :, None]
    wcode = jnp.sum(hits * jnp.arange(1, 3, dtype=jnp.int32)[None, :, None], axis=1).reshape(-1)

    def turn(d):
        return [(order[i] * 2 + c, order[(i + d) % chips] * 2 + c) for i in range(chips) for c in range(2)]

    def shift(x, d):
        return lax.ppermute(x, "row", turn(d))

    def twin(x):
        return lax.ppermute(x, "row", [(i, i ^ 1) for i in range(number)])

    around = chip_at[(my_position + jnp.arange(chips, dtype=jnp.int32)) % chips]
    meta = jnp.concatenate([core[None], around, me[None]]).astype(jnp.int32)
    held = load(meta, wcode, integrals)

    left = right = amps
    depth = integrals.shape[2] // number
    message_rows = chips * depth + -(-chips // CODE_ROWS) * CODE_ROWS
    chain, codes, order_of = [], [], []

    def run(offsets, arrivals, last=False):
        nonlocal chain
        blocks = []
        for a in arrivals:
            blocks += [a, twin(a)] if not last else [*a, *[twin(x) for x in a]]
        offsets = [o % chips for o in offsets]
        out = ladder(
            offsets, meta, wcode, blocks, held, chain, number, len(order_of) * depth, message_rows, codes if last else ()
        )
        chain = out[:2]
        codes.extend(out[2:])
        order_of.extend(offsets)

    run([0], [amps])
    for s in range(1, half):
        if s > 1:
            left, right, codes[-1] = lax.optimization_barrier((left, right, codes[-1]))
        before = left, right
        left, right = shift(left, 1), shift(right, -1)
        if s > 1:
            run([1 - s, s - 1], before)
    left, right, codes[-1] = lax.optimization_barrier((left, right, codes[-1]))
    final = shift(left[0, 0], 1), shift(right[0, 1], -1)
    run([1 - half, half - 1], [left, right])
    *final, codes[-1] = lax.optimization_barrier((*final, codes[-1]))
    run([half], [final], last=True)
    direct, message = chain
    received = lax.all_to_all(message, "row", split_axis=0, concat_axis=0, tiled=True)

    def places(chip, source):
        return order_of.index((position[chip] - position[source]) % chips)

    direct = direct.reshape(number, pair_rows, integrals.shape[2])
    return symmetrize(mirror, received, direct, places)


def solution(mesh):
    return jax.shard_map(
        functools.partial(local, ring_order(mesh)),
        mesh=mesh,
        in_specs=(
            P(("groups", "row"), None, None, None),
            P("groups", None, "row"),
            P("groups", None),
            P("groups", None),
            P("groups"),
        ),
        out_specs=P("groups", None, "row"),
        check_vma=False,
    )
```

```python
import functools

import jax
import jax.numpy as jnp
from jax import lax
from jax.experimental import pallas as pl
from jax.experimental.pallas import tpu as pltpu
from jax.sharding import PartitionSpec as P

OT = 8
LEVELS = 32767.0
STEPS_PER_OCTAVE = 64.0
CODE_ROWS = 16
CHUNK = 1024
SPAN = 128
LADDER_VMEM = 16 * 1024 * 1024
STREAM_VMEM = 32 * 1024 * 1024
SYMMETRIZE_VMEM = 24 * 1024 * 1024


def ring_order(mesh):
    size = mesh.shape["row"] // 2
    chips = [getattr(d, "coords", (0, 0, n)) for n, d in enumerate(mesh.devices[0, ::2])]
    columns = sorted({c[1] for c in chips})
    order = sorted(range(size), key=lambda n: (chips[n][1], chips[n][2]))
    if len(columns) == 2:
        half = size // 2
        order = order[:half] + order[half:][::-1]
    return order


def hbm(x):
    return pltpu.with_memory_space_constraint(x, pltpu.HBM)


def vmem(x):
    return pltpu.with_memory_space_constraint(x, pltpu.VMEM)


def load_kernel(meta, wcode, source, target, sem):
    copies = [pltpu.make_async_copy(source.at[t], target.at[t], sem.at[t]) for t in range(source.shape[0])]
    for copy in copies:
        copy.start()
    for copy in copies:
        copy.wait()


def load(meta, wcode, integrals):
    return pl.pallas_call(
        load_kernel,
        in_specs=[
            pl.BlockSpec(memory_space=pltpu.SMEM),
            pl.BlockSpec(memory_space=pltpu.SMEM),
            pl.BlockSpec(memory_space=pl.ANY),
        ],
        out_specs=pl.BlockSpec(memory_space=pltpu.VMEM),
        out_shape=pltpu.VMEM(integrals.shape, integrals.dtype),
        scratch_shapes=[pltpu.SemaphoreType.DMA((integrals.shape[0],))],
        compiler_params=pltpu.CompilerParams(vmem_limit_bytes=4 * 1024 * 1024),
        name="load",
    )(meta, wcode, hbm(integrals))


def ladder_kernel(offsets, start_row, earlier, chained, stream, pair_rows, meta, wcode, *refs):
    slots, last = len(offsets), earlier > 0
    if last:
        blocks, refs = refs[:4], refs[4:]
        views = [[(blocks[0], blocks[1]), (blocks[2], blocks[3])]]
    else:
        blocks, refs = refs[: 2 * slots], refs[2 * slots :]
        views = [[(b.at[0, 0], b.at[0, 1]) for b in blocks[2 * u : 2 * u + 2]] for u in range(slots)]
    integrals, refs = refs[0], refs[1:]
    before, refs = refs[:earlier], refs[earlier:]
    direct, *outs, acc, turned, coded, sem = refs[chained:]
    step = pl.program_id(0)
    tiles, _, columns = integrals.shape
    core = meta[0]
    height = 2 * pair_rows
    cores = core, 1 - core

    def product(at, part):
        total = None
        for t in range(tiles):
            rows = []
            for u in range(slots):
                for c in range(2):
                    code = wcode[(meta[1 + offsets[u]] * 2 + cores[c]) * tiles + t]
                    a0, a1 = (view[:, pl.ds(at, CHUNK)] for view in views[u][c])
                    rows.append(jnp.where(code == 1, a0, jnp.where(code == 2, a1, jnp.zeros_like(a0))))
            term = jnp.dot(jnp.concatenate(rows, axis=0), part[t], preferred_element_type=jnp.float32)
            total = term if total is None else total + term
        return total

    if stream:

        @pl.when(step == 0)
        def _():
            acc[...] = jnp.zeros_like(acc)

        acc[...] += product(pl.multiple_of(step * CHUNK, CHUNK), integrals)
    else:
        for k in range(integrals.shape[1] // CHUNK):
            term = product(k * CHUNK, integrals.at[:, k * CHUNK : (k + 1) * CHUNK, :])
            acc[...] = acc[...] + term if k else term

    @pl.when(step == pl.num_programs(0) - 1)
    def _():
        total = acc[...]
        copies = []
        for u in range(slots):
            for c in range(2):
                at = u * height + cores[c] * pair_rows
                rows = slice(u * height + c * pair_rows, u * height + (c + 1) * pair_rows)
                acc[pl.ds(pl.multiple_of(at, pair_rows), pair_rows), :] = total[rows, :]
            start = pl.multiple_of(meta[1 + offsets[u]] * height, height)
            copies.append(
                pltpu.make_async_copy(
                    acc.at[pl.ds(u * height, height), :], direct.at[pl.ds(start, height), :], sem.at[u]
                )
            )
            copies[-1].start()
        local_rows = columns // SPAN
        number = coded.shape[0]
        depth = columns // number
        for u in range(slots):
            for a in range(local_rows):
                piece = acc[u * height : (u + 1) * height, a * SPAN : (a + 1) * SPAN]
                turned[pl.ds(a, SPAN, stride=local_rows), :] = piece.T
            values = turned[...]
            largest = jnp.max(jnp.abs(values), axis=0, keepdims=True)
            code = jnp.ceil(jnp.log2(jnp.maximum(largest, 1e-30)) * STEPS_PER_OCTAVE) + 1.0
            scale = jnp.exp2(code * (-1.0 / STEPS_PER_OCTAVE)) * LEVELS
            whole = jnp.round(values * scale).astype(jnp.int32).astype(jnp.int16)
            coded[:, u * depth : (u + 1) * depth, :] = whole.reshape(number, depth, height)
            if last:
                rows = [*[r[...] for r in before], code.astype(jnp.int32)]
                spare = coded.shape[1] - depth - sum(r.shape[0] for r in rows)
                if spare:
                    rows.append(jnp.zeros((spare, height), jnp.int32))
                table = jnp.concatenate(rows, axis=0).astype(jnp.int16)
                coded[:, depth:, :] = jnp.broadcast_to(table[None], (number, *table.shape))
            else:
                outs[1][u : u + 1, :] = code.astype(jnp.int32)
        if last:
            chips = number // 2
            for k in range(chips):
                pair = pl.ds((meta[1] + k) % chips * 2, 2)
                copies.append(pltpu.make_async_copy(coded.at[pair], outs[k], sem.at[slots + k]))
                copies[-1].start()
        else:
            target = outs[0].at[:, pl.ds(start_row, coded.shape[1]), :]
            copies.append(pltpu.make_async_copy(coded, target, sem.at[slots]))
            copies[-1].start()
        for copy in copies:
            copy.wait()


def ladder(offsets, meta, wcode, blocks, integrals, stream, chain, number, start_row, message_rows, earlier=()):
    slots = len(offsets)
    pair_rows, cd_width = blocks[0].shape[-2:]
    tiles, _, columns = integrals.shape
    last = len(earlier) > 0
    depth = columns // number
    height = 2 * pair_rows
    rows = slots * depth
    if last:
        rows += -(-(sum(c.shape[0] for c in earlier) + 1) // CODE_ROWS) * CODE_ROWS
    in_specs = [pl.BlockSpec(memory_space=pltpu.VMEM) for _ in blocks]
    if stream:
        in_specs.append(pl.BlockSpec((tiles, CHUNK, columns), lambda k, *_: (0, k, 0)))
        integrals = hbm(integrals)
    else:
        in_specs.append(pl.BlockSpec(memory_space=pltpu.VMEM))
        integrals = vmem(integrals)
    operands = [meta, wcode, *[vmem(b) for b in blocks], integrals]
    for code in earlier:
        in_specs.append(pl.BlockSpec(memory_space=pltpu.VMEM))
        operands.append(code)
    aliases = {}
    for n, array in enumerate(chain):
        in_specs.append(pl.BlockSpec(memory_space=pl.ANY))
        aliases[len(operands)] = n
        operands.append(hbm(array))
    out_shape = [pltpu.HBM((number * pair_rows, columns), jnp.float32)]
    if last:
        out_shape += [pltpu.HBM((2, rows, height), jnp.int16)] * (number // 2)
    else:
        out_shape.append(pltpu.HBM((number, message_rows, height), jnp.int16))
    out_specs = [pl.BlockSpec(memory_space=pl.ANY)] * len(out_shape)
    if not last:
        out_specs.append(pl.BlockSpec((slots, height), lambda k, *_: (0, 0)))
        out_shape.append(jax.ShapeDtypeStruct((slots, height), jnp.int32))
    flops = 2 * slots * height * tiles * cd_width * columns
    return pl.pallas_call(
        functools.partial(ladder_kernel, offsets, start_row, len(earlier), len(chain), stream, pair_rows),
        grid_spec=pltpu.PrefetchScalarGridSpec(
            num_scalar_prefetch=2,
            grid=(cd_width // CHUNK if stream else 1,),
            in_specs=in_specs,
            out_specs=out_specs,
            scratch_shapes=[
                pltpu.VMEM((slots * height, columns), jnp.float32),
                pltpu.VMEM((columns, height), jnp.float32),
                pltpu.VMEM((number, rows, height), jnp.int16),
                pltpu.SemaphoreType.DMA((slots + (number // 2 if last else 1),)),
            ],
        ),
        out_shape=out_shape,
        input_output_aliases=aliases,
        compiler_params=pltpu.CompilerParams(vmem_limit_bytes=STREAM_VMEM if stream else LADDER_VMEM),
        cost_estimate=pl.CostEstimate(flops=flops, bytes_accessed=1 << 20, transcendentals=0),
        name=f"ladder{slots}",
    )(*operands)


def symmetrize_kernel(places, local_rows, pair_rows, mirror, meta, early, late, *refs):
    *pieces, direct, residual, own, rounded, turned, tail, in_sem, out_sem, tail_sem = refs
    core = meta[0]
    moves = []
    for n, piece in enumerate(pieces):
        k, other = n // 2, n % 2
        chips = len(pieces) // 2
        source = (meta[1] + chips - k) % chips * 2 + (1 - core if other else core)
        moves.append(pltpu.make_async_copy(piece.at[core], tail.at[source], tail_sem.at[n]))
        moves[-1].start()
    number, columns = own.shape[0], own.shape[2]
    chips = number // 2
    height = 2 * pair_rows
    depth = local_rows * local_rows
    loads, stores = [], []
    for m in range(number):
        p = mirror[m]
        loads.append(pltpu.make_async_copy(direct.at[p], own.at[m], in_sem.at[m]))
        stores.append(pltpu.make_async_copy(rounded.at[m], residual.at[p], out_sem.at[m]))
        loads[m].start()
    row = lax.broadcasted_iota(jnp.int32, (height, height), 0)
    lane = lax.broadcasted_iota(jnp.int32, (height, height), 1)
    inner = row % pair_rows
    partner = row - inner + (inner % OT) * OT + inner // OT
    pick = jnp.where(lane == partner, 1.0, 0.0).astype(jnp.bfloat16)
    pick = jnp.concatenate([pick, pick], axis=1)
    for move in moves:
        move.wait()
    scales = []
    for i in range(number):
        code = tail[i, depth:, :].astype(jnp.int32).astype(jnp.float32)
        scales.append(jnp.exp2(code * (1.0 / STEPS_PER_OCTAVE)) * (1.0 / LEVELS))
    for chip in range(chips):
        for i in range(number):
            place = places(chip, i // 2)
            split = early.shape[1] // depth
            if place < split:
                whole = early[i, place * depth : (place + 1) * depth, :]
            elif place < chips - 1:
                whole = late[i, (place - split) * depth : (place - split + 1) * depth, :]
            else:
                whole = tail[i, :depth, :]
            whole = whole.astype(jnp.int32).astype(jnp.float32)
            whole = whole * scales[i][place : place + 1, :]
            for b in range(local_rows):
                at = (b * number + i) * local_rows
                turned[at : at + local_rows, :] = whole[b * local_rows : (b + 1) * local_rows, :]
        values = turned[...]
        high = values.astype(jnp.bfloat16)
        low = (values - high.astype(jnp.float32)).astype(jnp.bfloat16)
        both = jnp.concatenate([high, low], axis=1)
        mirrored = lax.dot_general(pick, both, (((1,), (1,)), ((), ())), preferred_element_type=jnp.float32)
        for h in range(2):
            m = chip * 2 + h
            loads[m].wait()
            rounded[m] = (own[m] + mirrored[h * pair_rows : (h + 1) * pair_rows, :]).astype(jnp.bfloat16)
            stores[m].start()
    for m in range(number):
        stores[m].wait()


def symmetrize(mirror, meta, early, late, pieces, direct, places):
    number, pair_rows, columns = direct.shape
    local_rows = columns // SPAN
    height = 2 * pair_rows
    return pl.pallas_call(
        functools.partial(symmetrize_kernel, places, local_rows, pair_rows),
        in_specs=[
            pl.BlockSpec(memory_space=pltpu.SMEM),
            pl.BlockSpec(memory_space=pltpu.SMEM),
            pl.BlockSpec(memory_space=pltpu.VMEM),
            pl.BlockSpec(memory_space=pltpu.VMEM),
            *[pl.BlockSpec(memory_space=pl.ANY) for _ in pieces],
            pl.BlockSpec(memory_space=pl.ANY),
        ],
        out_specs=pl.BlockSpec(memory_space=pl.ANY),
        out_shape=jax.ShapeDtypeStruct(direct.shape, jnp.bfloat16),
        scratch_shapes=[
            pltpu.VMEM(direct.shape, jnp.float32),
            pltpu.VMEM(direct.shape, jnp.bfloat16),
            pltpu.VMEM((columns, height), jnp.float32),
            pltpu.VMEM((number, *pieces[0].shape[1:]), jnp.int16),
            pltpu.SemaphoreType.DMA((number,)),
            pltpu.SemaphoreType.DMA((number,)),
            pltpu.SemaphoreType.DMA((number,)),
        ],
        compiler_params=pltpu.CompilerParams(vmem_limit_bytes=SYMMETRIZE_VMEM),
        cost_estimate=pl.CostEstimate(flops=0, bytes_accessed=direct.size * 8, transcendentals=0),
        name="symmetrize",
    )(mirror, meta, early, late, *pieces, hbm(direct))


def local(order, amps, integrals, domain_mask, tile_list, mirror):
    number = mirror.shape[0]
    pair_rows, cd_width = amps.shape[2:]
    tiles = integrals.shape[0]
    chips = len(order)
    half = chips // 2
    position = [order.index(c) for c in range(chips)]
    me = lax.axis_index("row")
    my_position = jnp.array(position, jnp.int32)[me // 2]
    chip_at = jnp.array(order, jnp.int32)
    core = me % 2

    alive = jnp.take_along_axis(domain_mask, tile_list, axis=1)
    which = jnp.arange(tiles, dtype=jnp.int32)
    hits = (tile_list[:, :, None] == which) * alive[:, :, None]
    wcode = jnp.sum(hits * jnp.arange(1, 3, dtype=jnp.int32)[None, :, None], axis=1).reshape(-1)

    def turn(d):
        return [(order[i] * 2 + c, order[(i + d) % chips] * 2 + c) for i in range(chips) for c in range(2)]

    def shift(x, d):
        return lax.ppermute(x, "row", turn(d))

    def twin(x):
        return lax.ppermute(x, "row", [(i, i ^ 1) for i in range(number)])

    around = chip_at[(my_position + jnp.arange(chips, dtype=jnp.int32)) % chips]
    meta = jnp.concatenate([core[None], around, me[None]]).astype(jnp.int32)
    held = load(meta, wcode, integrals)

    left = right = amps
    depth = integrals.shape[2] // number
    split = half // 2 * 2 - 1
    chain, early, codes, order_of = [], [], [], []

    def run(offsets, arrivals, last=False):
        nonlocal chain
        blocks = []
        for a in arrivals:
            blocks += [a, twin(a)] if not last else [*a, *[twin(x) for x in a]]
        offsets = [o % chips for o in offsets]
        if last:
            order_of.extend(offsets)
            return ladder(offsets, meta, wcode, blocks, integrals, True, chain[:1], number, 0, 0, codes)
        late = len(order_of) >= split
        if len(order_of) == split:
            early.append(chain.pop())
        start = (len(order_of) - split if late else len(order_of)) * depth
        rows = (chips - 1 - split if late else split) * depth
        out = ladder(offsets, meta, wcode, blocks, integrals if late else held, late, chain, number, start, rows)
        chain = list(out[:2])
        codes.extend(out[2:])
        order_of.extend(offsets)

    run([0], [amps])
    for s in range(1, half):
        if s > 1:
            left, right, codes[-1] = lax.optimization_barrier((left, right, codes[-1]))
        before = left, right
        left, right = shift(left, 1), shift(right, -1)
        if s > 1:
            run([1 - s, s - 1], before)
    left, right, codes[-1] = lax.optimization_barrier((left, right, codes[-1]))
    final = shift(left[0, 0], 1), shift(right[0, 1], -1)
    run([1 - half, half - 1], [left, right])
    *final, chain[1] = lax.optimization_barrier((*final, chain[1]))
    direct, *tail = run([half], [final], last=True)
    bulk = [
        lax.all_to_all(m, "row", split_axis=0, concat_axis=0, tiled=True) for m in (early[0], chain[1])
    ]
    pieces = []
    for k in range(chips):
        ahead = [(i, (i + 2 * k) % number) for i in range(number)]
        piece = lax.ppermute(tail[k], "row", ahead) if k else tail[0]
        pieces += [piece, twin(piece)]

    def places(chip, source):
        return order_of.index((position[chip] - position[source]) % chips)

    direct = direct.reshape(number, pair_rows, integrals.shape[2])
    return symmetrize(mirror, meta, *bulk, pieces, direct, places)


def solution(mesh):
    return jax.shard_map(
        functools.partial(local, ring_order(mesh)),
        mesh=mesh,
        in_specs=(
            P(("groups", "row"), None, None, None),
            P("groups", None, "row"),
            P("groups", None),
            P("groups", None),
            P("groups"),
        ),
        out_specs=P("groups", None, "row"),
        check_vma=False,
    )
```

```python
import functools

import jax
import jax.numpy as jnp
from jax import lax
from jax.experimental import pallas as pl
from jax.experimental.pallas import tpu as pltpu
from jax.sharding import PartitionSpec as P

OT = 8
LEVELS = 32767.0
STEPS_PER_OCTAVE = 64.0
CODE_ROWS = 16
CHUNK = 1024
SPAN = 128
LADDER_VMEM = 16 * 1024 * 1024
STREAM_VMEM = 32 * 1024 * 1024
SYMMETRIZE_VMEM = 24 * 1024 * 1024


def ring_order(mesh):
    size = mesh.shape["row"] // 2
    chips = [getattr(d, "coords", (0, 0, n)) for n, d in enumerate(mesh.devices[0, ::2])]
    columns = sorted({c[1] for c in chips})
    order = sorted(range(size), key=lambda n: (chips[n][1], chips[n][2]))
    if len(columns) == 2:
        half = size // 2
        order = order[:half] + order[half:][::-1]
    return order, chips


def shortcuts(order, places):
    size = len(order)

    def near(r, q):
        pair = places[order[r]], places[order[q % size]]
        return sum(abs(a - b) for a, b in zip(*pair)) == 1

    from_left = [r for r in range(size) if near(r, r + size // 2 + 1)]
    from_right = [r for r in range(size) if near(r, r + size // 2 - 1)]
    return from_left, from_right


def hbm(x):
    return pltpu.with_memory_space_constraint(x, pltpu.HBM)


def vmem(x):
    return pltpu.with_memory_space_constraint(x, pltpu.VMEM)


def load_kernel(meta, wcode, source, target, sem):
    copies = [pltpu.make_async_copy(source.at[t], target.at[t], sem.at[t]) for t in range(source.shape[0])]
    for copy in copies:
        copy.start()
    for copy in copies:
        copy.wait()


def load(meta, wcode, integrals):
    return pl.pallas_call(
        load_kernel,
        in_specs=[
            pl.BlockSpec(memory_space=pltpu.SMEM),
            pl.BlockSpec(memory_space=pltpu.SMEM),
            pl.BlockSpec(memory_space=pl.ANY),
        ],
        out_specs=pl.BlockSpec(memory_space=pltpu.VMEM),
        out_shape=pltpu.VMEM(integrals.shape, integrals.dtype),
        scratch_shapes=[pltpu.SemaphoreType.DMA((integrals.shape[0],))],
        compiler_params=pltpu.CompilerParams(vmem_limit_bytes=4 * 1024 * 1024),
        name="load",
    )(meta, wcode, hbm(integrals))


def ladder_kernel(relayed, offsets, start_row, earlier, chained, stream, pair_rows, meta, wcode, *refs):
    slots, last = len(offsets), earlier > 0
    if last:
        blocks, refs = refs[:4], refs[4:]
        views = [[(blocks[0], blocks[1]), (blocks[2], blocks[3])]]
    else:
        blocks, refs = refs[: 2 * slots], refs[2 * slots :]
        views = [[(b.at[0, 0], b.at[0, 1]) for b in blocks[2 * u : 2 * u + 2]] for u in range(slots)]
    relays = ()
    if last and relayed:
        relays, refs = refs[:2], refs[2:]
    integrals, refs = refs[0], refs[1:]
    before, refs = refs[:earlier], refs[earlier:]
    direct, *outs, acc, turned, coded, sem = refs[chained:]
    step = pl.program_id(0)
    tiles, _, columns = integrals.shape
    core = meta[0]
    height = 2 * pair_rows
    cores = core, 1 - core
    flag = meta[meta.shape[0] - 1]

    def product(at, part):
        total = None
        for t in range(tiles):
            rows = []
            for u in range(slots):
                for c in range(2):
                    code = wcode[(meta[1 + offsets[u]] * 2 + cores[c]) * tiles + t]
                    a0, a1 = (view[:, pl.ds(at, CHUNK)] for view in views[u][c])
                    if relays:
                        b0, b1 = (relays[c][0, k, :, pl.ds(at, CHUNK)] for k in range(2))
                        a0, a1 = jnp.where(flag == 1, b0, a0), jnp.where(flag == 1, b1, a1)
                    rows.append(jnp.where(code == 1, a0, jnp.where(code == 2, a1, jnp.zeros_like(a0))))
            term = jnp.dot(jnp.concatenate(rows, axis=0), part[t], preferred_element_type=jnp.float32)
            total = term if total is None else total + term
        return total

    if stream:

        @pl.when(step == 0)
        def _():
            acc[...] = jnp.zeros_like(acc)

        acc[...] += product(pl.multiple_of(step * CHUNK, CHUNK), integrals)
    else:
        for k in range(integrals.shape[1] // CHUNK):
            term = product(k * CHUNK, integrals.at[:, k * CHUNK : (k + 1) * CHUNK, :])
            acc[...] = acc[...] + term if k else term

    @pl.when(step == pl.num_programs(0) - 1)
    def _():
        total = acc[...]
        copies = []
        for u in range(slots):
            for c in range(2):
                at = u * height + cores[c] * pair_rows
                rows = slice(u * height + c * pair_rows, u * height + (c + 1) * pair_rows)
                acc[pl.ds(pl.multiple_of(at, pair_rows), pair_rows), :] = total[rows, :]
            start = pl.multiple_of(meta[1 + offsets[u]] * height, height)
            copies.append(
                pltpu.make_async_copy(
                    acc.at[pl.ds(u * height, height), :], direct.at[pl.ds(start, height), :], sem.at[u]
                )
            )
            copies[-1].start()
        local_rows = columns // SPAN
        number = coded.shape[0]
        depth = columns // number
        for u in range(slots):
            for a in range(local_rows):
                piece = acc[u * height : (u + 1) * height, a * SPAN : (a + 1) * SPAN]
                turned[pl.ds(a, SPAN, stride=local_rows), :] = piece.T
            values = turned[...]
            largest = jnp.max(jnp.abs(values), axis=0, keepdims=True)
            code = jnp.ceil(jnp.log2(jnp.maximum(largest, 1e-30)) * STEPS_PER_OCTAVE) + 1.0
            scale = jnp.exp2(code * (-1.0 / STEPS_PER_OCTAVE)) * LEVELS
            whole = jnp.round(values * scale).astype(jnp.int32).astype(jnp.int16)
            coded[:, u * depth : (u + 1) * depth, :] = whole.reshape(number, depth, height)
            if last:
                rows = [*[r[...] for r in before], code.astype(jnp.int32)]
                spare = coded.shape[1] - depth - sum(r.shape[0] for r in rows)
                if spare:
                    rows.append(jnp.zeros((spare, height), jnp.int32))
                table = jnp.concatenate(rows, axis=0).astype(jnp.int16)
                coded[:, depth:, :] = jnp.broadcast_to(table[None], (number, *table.shape))
            else:
                outs[1][u : u + 1, :] = code.astype(jnp.int32)
        if last:
            chips = number // 2
            for k in range(chips):
                pair = pl.ds((meta[1] + k) % chips * 2, 2)
                copies.append(pltpu.make_async_copy(coded.at[pair], outs[k], sem.at[slots + k]))
                copies[-1].start()
        else:
            target = outs[0].at[:, pl.ds(start_row, coded.shape[1]), :]
            copies.append(pltpu.make_async_copy(coded, target, sem.at[slots]))
            copies[-1].start()
        for copy in copies:
            copy.wait()


def ladder(offsets, meta, wcode, blocks, integrals, stream, chain, number, start_row, message_rows, earlier=()):
    slots = len(offsets)
    pair_rows, cd_width = blocks[0].shape[-2:]
    tiles, _, columns = integrals.shape
    last = len(earlier) > 0
    depth = columns // number
    height = 2 * pair_rows
    rows = slots * depth
    if last:
        rows += -(-(sum(c.shape[0] for c in earlier) + 1) // CODE_ROWS) * CODE_ROWS
    in_specs = [pl.BlockSpec(memory_space=pltpu.VMEM) for _ in blocks]
    if stream:
        in_specs.append(pl.BlockSpec((tiles, CHUNK, columns), lambda k, *_: (0, k, 0)))
        integrals = hbm(integrals)
    else:
        in_specs.append(pl.BlockSpec(memory_space=pltpu.VMEM))
        integrals = vmem(integrals)
    operands = [meta, wcode, *[vmem(b) for b in blocks], integrals]
    for code in earlier:
        in_specs.append(pl.BlockSpec(memory_space=pltpu.VMEM))
        operands.append(code)
    aliases = {}
    for n, array in enumerate(chain):
        in_specs.append(pl.BlockSpec(memory_space=pl.ANY))
        aliases[len(operands)] = n
        operands.append(hbm(array))
    out_shape = [pltpu.HBM((number * pair_rows, columns), jnp.float32)]
    if last:
        out_shape += [pltpu.HBM((2, rows, height), jnp.int16)] * (number // 2)
    else:
        out_shape.append(pltpu.HBM((number, message_rows, height), jnp.int16))
    out_specs = [pl.BlockSpec(memory_space=pl.ANY)] * len(out_shape)
    if not last:
        out_specs.append(pl.BlockSpec((slots, height), lambda k, *_: (0, 0)))
        out_shape.append(jax.ShapeDtypeStruct((slots, height), jnp.int32))
    flops = 2 * slots * height * tiles * cd_width * columns
    return pl.pallas_call(
        functools.partial(ladder_kernel, len(blocks) > 4 * slots, offsets, start_row, len(earlier), len(chain), stream, pair_rows),
        grid_spec=pltpu.PrefetchScalarGridSpec(
            num_scalar_prefetch=2,
            grid=(cd_width // CHUNK if stream else 1,),
            in_specs=in_specs,
            out_specs=out_specs,
            scratch_shapes=[
                pltpu.VMEM((slots * height, columns), jnp.float32),
                pltpu.VMEM((columns, height), jnp.float32),
                pltpu.VMEM((number, rows, height), jnp.int16),
                pltpu.SemaphoreType.DMA((slots + (number // 2 if last else 1),)),
            ],
        ),
        out_shape=out_shape,
        input_output_aliases=aliases,
        compiler_params=pltpu.CompilerParams(vmem_limit_bytes=STREAM_VMEM if stream else LADDER_VMEM),
        cost_estimate=pl.CostEstimate(flops=flops, bytes_accessed=1 << 20, transcendentals=0),
        name=f"ladder{slots}",
    )(*operands)


def symmetrize_kernel(places, local_rows, pair_rows, mirror, meta, early, late, *refs):
    *pieces, direct, residual, own, rounded, turned, tail, in_sem, out_sem, tail_sem = refs
    core = meta[0]
    moves = []
    for n, piece in enumerate(pieces):
        k, other = n // 2, n % 2
        chips = len(pieces) // 2
        source = (meta[1] + chips - k) % chips * 2 + (1 - core if other else core)
        moves.append(pltpu.make_async_copy(piece.at[core], tail.at[source], tail_sem.at[n]))
        moves[-1].start()
    number, columns = own.shape[0], own.shape[2]
    chips = number // 2
    height = 2 * pair_rows
    depth = local_rows * local_rows
    loads, stores = [], []
    for m in range(number):
        p = mirror[m]
        loads.append(pltpu.make_async_copy(direct.at[p], own.at[m], in_sem.at[m]))
        stores.append(pltpu.make_async_copy(rounded.at[m], residual.at[p], out_sem.at[m]))
        loads[m].start()
    row = lax.broadcasted_iota(jnp.int32, (height, height), 0)
    lane = lax.broadcasted_iota(jnp.int32, (height, height), 1)
    inner = row % pair_rows
    partner = row - inner + (inner % OT) * OT + inner // OT
    pick = jnp.where(lane == partner, 1.0, 0.0).astype(jnp.bfloat16)
    pick = jnp.concatenate([pick, pick], axis=1)
    for move in moves:
        move.wait()
    scales = []
    for i in range(number):
        code = tail[i, depth:, :].astype(jnp.int32).astype(jnp.float32)
        scales.append(jnp.exp2(code * (1.0 / STEPS_PER_OCTAVE)) * (1.0 / LEVELS))
    for chip in range(chips):
        for i in range(number):
            place = places(chip, i // 2)
            split = early.shape[1] // depth
            if place < split:
                whole = early[i, place * depth : (place + 1) * depth, :]
            elif place < chips - 1:
                whole = late[i, (place - split) * depth : (place - split + 1) * depth, :]
            else:
                whole = tail[i, :depth, :]
            whole = whole.astype(jnp.int32).astype(jnp.float32)
            whole = whole * scales[i][place : place + 1, :]
            for b in range(local_rows):
                at = (b * number + i) * local_rows
                turned[at : at + local_rows, :] = whole[b * local_rows : (b + 1) * local_rows, :]
        values = turned[...]
        high = values.astype(jnp.bfloat16)
        low = (values - high.astype(jnp.float32)).astype(jnp.bfloat16)
        both = jnp.concatenate([high, low], axis=1)
        mirrored = lax.dot_general(pick, both, (((1,), (1,)), ((), ())), preferred_element_type=jnp.float32)
        for h in range(2):
            m = chip * 2 + h
            loads[m].wait()
            rounded[m] = (own[m] + mirrored[h * pair_rows : (h + 1) * pair_rows, :]).astype(jnp.bfloat16)
            stores[m].start()
    for m in range(number):
        stores[m].wait()


def symmetrize(mirror, meta, early, late, pieces, direct, places):
    number, pair_rows, columns = direct.shape
    local_rows = columns // SPAN
    height = 2 * pair_rows
    return pl.pallas_call(
        functools.partial(symmetrize_kernel, places, local_rows, pair_rows),
        in_specs=[
            pl.BlockSpec(memory_space=pltpu.SMEM),
            pl.BlockSpec(memory_space=pltpu.SMEM),
            pl.BlockSpec(memory_space=pltpu.VMEM),
            pl.BlockSpec(memory_space=pltpu.VMEM),
            *[pl.BlockSpec(memory_space=pl.ANY) for _ in pieces],
            pl.BlockSpec(memory_space=pl.ANY),
        ],
        out_specs=pl.BlockSpec(memory_space=pl.ANY),
        out_shape=jax.ShapeDtypeStruct(direct.shape, jnp.bfloat16),
        scratch_shapes=[
            pltpu.VMEM(direct.shape, jnp.float32),
            pltpu.VMEM(direct.shape, jnp.bfloat16),
            pltpu.VMEM((columns, height), jnp.float32),
            pltpu.VMEM((number, *pieces[0].shape[1:]), jnp.int16),
            pltpu.SemaphoreType.DMA((number,)),
            pltpu.SemaphoreType.DMA((number,)),
            pltpu.SemaphoreType.DMA((number,)),
        ],
        compiler_params=pltpu.CompilerParams(vmem_limit_bytes=SYMMETRIZE_VMEM),
        cost_estimate=pl.CostEstimate(flops=0, bytes_accessed=direct.size * 8, transcendentals=0),
        name="symmetrize",
    )(mirror, meta, early, late, *pieces, hbm(direct))


def local(order, places_of, amps, integrals, domain_mask, tile_list, mirror):
    number = mirror.shape[0]
    pair_rows, cd_width = amps.shape[2:]
    tiles = integrals.shape[0]
    chips = len(order)
    half = chips // 2
    position = [order.index(c) for c in range(chips)]
    me = lax.axis_index("row")
    my_position = jnp.array(position, jnp.int32)[me // 2]
    chip_at = jnp.array(order, jnp.int32)
    core = me % 2

    alive = jnp.take_along_axis(domain_mask, tile_list, axis=1)
    which = jnp.arange(tiles, dtype=jnp.int32)
    hits = (tile_list[:, :, None] == which) * alive[:, :, None]
    wcode = jnp.sum(hits * jnp.arange(1, 3, dtype=jnp.int32)[None, :, None], axis=1).reshape(-1)

    def turn(d):
        return [(order[i] * 2 + c, order[(i + d) % chips] * 2 + c) for i in range(chips) for c in range(2)]

    def shift(x, d, without=()):
        pairs = turn(d)
        return lax.ppermute(x, "row", [p for p in pairs if position[p[1] // 2] not in without])

    def relay(x, targets, d):
        hop = [(order[(r + half + d) % chips], order[r]) for r in targets]
        return lax.ppermute(x, "row", [(a * 2 + c, b * 2 + c) for a, b in hop for c in range(2)])

    def twin(x):
        return lax.ppermute(x, "row", [(i, i ^ 1) for i in range(number)])

    around = chip_at[(my_position + jnp.arange(chips, dtype=jnp.int32)) % chips]
    from_left, from_right = shortcuts(order, places_of)
    skip = sorted(from_left + from_right)
    skips = jnp.array([r in skip for r in range(chips)], jnp.int32)[my_position]
    meta = jnp.concatenate([core[None], around, me[None], skips[None]]).astype(jnp.int32)
    held = load(meta, wcode, integrals)

    left = right = amps
    depth = integrals.shape[2] // number
    split = half // 2 * 2 - 1
    chain, early, codes, order_of = [], [], [], []

    def run(offsets, arrivals, last=False):
        nonlocal chain
        blocks = []
        for a in arrivals:
            blocks += [a, twin(a)] if not last else [*a, *[twin(x) for x in a]]
        if last and skip:
            blocks += [relayed, twin(relayed)]
        offsets = [o % chips for o in offsets]
        if last:
            order_of.extend(offsets)
            return ladder(offsets, meta, wcode, blocks, integrals, True, chain[:1], number, 0, 0, codes)
        late = len(order_of) >= split
        if len(order_of) == split:
            early.append(chain.pop())
        start = (len(order_of) - split if late else len(order_of)) * depth
        rows = (chips - 1 - split if late else split) * depth
        out = ladder(offsets, meta, wcode, blocks, integrals if late else held, late, chain, number, start, rows)
        chain = list(out[:2])
        codes.extend(out[2:])
        order_of.extend(offsets)

    run([0], [amps])
    for s in range(1, half):
        if s > 1:
            left, right, codes[-1] = lax.optimization_barrier((left, right, codes[-1]))
        before = left, right
        left, right = shift(left, 1), shift(right, -1)
        if s == 1:
            nearest = left, right
        if s > 1:
            run([1 - s, s - 1], before)
    if skip:
        relayed = relay(nearest[0], from_left, 1) + relay(nearest[1], from_right, -1)
        left, right, relayed, codes[-1] = lax.optimization_barrier((left, right, relayed, codes[-1]))
    else:
        left, right, codes[-1] = lax.optimization_barrier((left, right, codes[-1]))
    final = shift(left[0, 0], 1, skip), shift(right[0, 1], -1, skip)
    run([1 - half, half - 1], [left, right])
    *final, chain[1] = lax.optimization_barrier((*final, chain[1]))
    direct, *tail = run([half], [final], last=True)
    bulk = [
        lax.all_to_all(m, "row", split_axis=0, concat_axis=0, tiled=True) for m in (early[0], chain[1])
    ]
    pieces = []
    for k in range(chips):
        ahead = [(i, (i + 2 * k) % number) for i in range(number)]
        piece = lax.ppermute(tail[k], "row", ahead) if k else tail[0]
        pieces += [piece, twin(piece)]

    def places(chip, source):
        return order_of.index((position[chip] - position[source]) % chips)

    direct = direct.reshape(number, pair_rows, integrals.shape[2])
    return symmetrize(mirror, meta, *bulk, pieces, direct, places)


def solution(mesh):
    return jax.shard_map(
        functools.partial(local, *ring_order(mesh)),
        mesh=mesh,
        in_specs=(
            P(("groups", "row"), None, None, None),
            P("groups", None, "row"),
            P("groups", None),
            P("groups", None),
            P("groups"),
        ),
        out_specs=P("groups", None, "row"),
        check_vma=False,
    )
```

```python
import functools

import jax
import jax.numpy as jnp
from jax import lax
from jax.experimental import pallas as pl
from jax.experimental.pallas import tpu as pltpu
from jax.sharding import PartitionSpec as P

OT = 8
LEVELS = 32768.0
MARGIN = 1.0 / 256
CODE_ROWS = 16
CHUNK = 1024
SPAN = 128
LADDER_VMEM = 16 * 1024 * 1024
STREAM_VMEM = 32 * 1024 * 1024
SYMMETRIZE_VMEM = 24 * 1024 * 1024


def ring_order(mesh):
    size = mesh.shape["row"] // 2
    chips = [getattr(d, "coords", (0, 0, n)) for n, d in enumerate(mesh.devices[0, ::2])]
    columns = sorted({c[1] for c in chips})
    order = sorted(range(size), key=lambda n: (chips[n][1], chips[n][2]))
    if len(columns) == 2:
        half = size // 2
        order = order[:half] + order[half:][::-1]
    return order, chips


def shortcuts(order, places):
    size = len(order)

    def near(r, q):
        pair = places[order[r]], places[order[q % size]]
        return sum(abs(a - b) for a, b in zip(*pair)) == 1

    from_left = [r for r in range(size) if near(r, r + size // 2 + 1)]
    from_right = [r for r in range(size) if near(r, r + size // 2 - 1)]
    return from_left, from_right


def hbm(x):
    return pltpu.with_memory_space_constraint(x, pltpu.HBM)


def vmem(x):
    return pltpu.with_memory_space_constraint(x, pltpu.VMEM)


def load_kernel(meta, wcode, source, target, sem):
    copies = [pltpu.make_async_copy(source.at[t], target.at[t], sem.at[t]) for t in range(source.shape[0])]
    for copy in copies:
        copy.start()
    for copy in copies:
        copy.wait()


def load(meta, wcode, integrals):
    return pl.pallas_call(
        load_kernel,
        in_specs=[
            pl.BlockSpec(memory_space=pltpu.SMEM),
            pl.BlockSpec(memory_space=pltpu.SMEM),
            pl.BlockSpec(memory_space=pl.ANY),
        ],
        out_specs=pl.BlockSpec(memory_space=pltpu.VMEM),
        out_shape=pltpu.VMEM(integrals.shape, integrals.dtype),
        scratch_shapes=[pltpu.SemaphoreType.DMA((integrals.shape[0],))],
        compiler_params=pltpu.CompilerParams(vmem_limit_bytes=4 * 1024 * 1024),
        name="load",
    )(meta, wcode, hbm(integrals))


def ladder_kernel(relayed, offsets, start_row, earlier, chained, stream, pair_rows, meta, wcode, *refs):
    slots, last = len(offsets), earlier > 0
    if last:
        blocks, refs = refs[:4], refs[4:]
        views = [[(blocks[0], blocks[1]), (blocks[2], blocks[3])]]
    else:
        blocks, refs = refs[: 2 * slots], refs[2 * slots :]
        views = [[(b.at[0, 0], b.at[0, 1]) for b in blocks[2 * u : 2 * u + 2]] for u in range(slots)]
    relays = ()
    if last and relayed:
        relays, refs = refs[:2], refs[2:]
    integrals, refs = refs[0], refs[1:]
    before, refs = refs[:earlier], refs[earlier:]
    direct, *outs, acc, turned, coded, sem = refs[chained:]
    step = pl.program_id(0)
    tiles, _, columns = integrals.shape
    core = meta[0]
    height = 2 * pair_rows
    cores = core, 1 - core
    flag = meta[meta.shape[0] - 1]

    def product(at, part):
        total = None
        for t in range(tiles):
            rows = []
            for u in range(slots):
                for c in range(2):
                    code = wcode[(meta[1 + offsets[u]] * 2 + cores[c]) * tiles + t]
                    a0, a1 = (view[:, pl.ds(at, CHUNK)] for view in views[u][c])
                    if relays:
                        b0, b1 = (relays[c][0, k, :, pl.ds(at, CHUNK)] for k in range(2))
                        a0, a1 = jnp.where(flag == 1, b0, a0), jnp.where(flag == 1, b1, a1)
                    rows.append(jnp.where(code == 1, a0, jnp.where(code == 2, a1, jnp.zeros_like(a0))))
            term = jnp.dot(jnp.concatenate(rows, axis=0), part[t], preferred_element_type=jnp.float32)
            total = term if total is None else total + term
        return total

    if stream:

        @pl.when(step == 0)
        def _():
            acc[...] = jnp.zeros_like(acc)

        acc[...] += product(pl.multiple_of(step * CHUNK, CHUNK), integrals)
    else:
        for k in range(integrals.shape[1] // CHUNK):
            term = product(k * CHUNK, integrals.at[:, k * CHUNK : (k + 1) * CHUNK, :])
            acc[...] = acc[...] + term if k else term

    @pl.when(step == pl.num_programs(0) - 1)
    def _():
        total = acc[...]
        copies = []
        for u in range(slots):
            for c in range(2):
                at = u * height + cores[c] * pair_rows
                rows = slice(u * height + c * pair_rows, u * height + (c + 1) * pair_rows)
                acc[pl.ds(pl.multiple_of(at, pair_rows), pair_rows), :] = total[rows, :]
            start = pl.multiple_of(meta[1 + offsets[u]] * height, height)
            copies.append(
                pltpu.make_async_copy(
                    acc.at[pl.ds(u * height, height), :], direct.at[pl.ds(start, height), :], sem.at[u]
                )
            )
            copies[-1].start()
        local_rows = columns // SPAN
        number = coded.shape[0]
        depth = columns // number
        for u in range(slots):
            for a in range(local_rows):
                piece = acc[u * height : (u + 1) * height, a * SPAN : (a + 1) * SPAN]
                turned[pl.ds(a, SPAN, stride=local_rows), :] = piece.T
            values = turned[...]
            largest = jnp.max(jnp.abs(values), axis=0, keepdims=True)
            code = jnp.ceil(jnp.log2(jnp.maximum(largest, 1e-30)) + MARGIN)
            scale = jnp.exp2(-code) * LEVELS
            whole = jnp.round(values * scale).astype(jnp.int32).astype(jnp.int16)
            coded[:, u * depth : (u + 1) * depth, :] = whole.reshape(number, depth, height)
            if last:
                rows = [*[r[...] for r in before], code.astype(jnp.int32)]
                spare = coded.shape[1] - depth - sum(r.shape[0] for r in rows)
                if spare:
                    rows.append(jnp.zeros((spare, height), jnp.int32))
                table = jnp.concatenate(rows, axis=0).astype(jnp.int16)
                coded[:, depth:, :] = jnp.broadcast_to(table[None], (number, *table.shape))
            else:
                outs[1][u : u + 1, :] = code.astype(jnp.int32)
        if last:
            chips = number // 2
            for k in range(chips):
                pair = pl.ds((meta[1] + k) % chips * 2, 2)
                copies.append(pltpu.make_async_copy(coded.at[pair], outs[k], sem.at[slots + k]))
                copies[-1].start()
        else:
            target = outs[0].at[:, pl.ds(start_row, coded.shape[1]), :]
            copies.append(pltpu.make_async_copy(coded, target, sem.at[slots]))
            copies[-1].start()
        for copy in copies:
            copy.wait()


def ladder(offsets, meta, wcode, blocks, integrals, stream, chain, number, start_row, message_rows, earlier=()):
    slots = len(offsets)
    pair_rows, cd_width = blocks[0].shape[-2:]
    tiles, _, columns = integrals.shape
    last = len(earlier) > 0
    depth = columns // number
    height = 2 * pair_rows
    rows = slots * depth
    if last:
        rows += -(-(sum(c.shape[0] for c in earlier) + 1) // CODE_ROWS) * CODE_ROWS
    in_specs = [pl.BlockSpec(memory_space=pltpu.VMEM) for _ in blocks]
    if stream:
        in_specs.append(pl.BlockSpec((tiles, CHUNK, columns), lambda k, *_: (0, k, 0)))
        integrals = hbm(integrals)
    else:
        in_specs.append(pl.BlockSpec(memory_space=pltpu.VMEM))
        integrals = vmem(integrals)
    operands = [meta, wcode, *[vmem(b) for b in blocks], integrals]
    for code in earlier:
        in_specs.append(pl.BlockSpec(memory_space=pltpu.VMEM))
        operands.append(code)
    aliases = {}
    for n, array in enumerate(chain):
        in_specs.append(pl.BlockSpec(memory_space=pl.ANY))
        aliases[len(operands)] = n
        operands.append(hbm(array))
    out_shape = [pltpu.HBM((number * pair_rows, columns), jnp.float32)]
    if last:
        out_shape += [pltpu.HBM((2, rows, height), jnp.int16)] * (number // 2)
    else:
        out_shape.append(pltpu.HBM((number, message_rows, height), jnp.int16))
    out_specs = [pl.BlockSpec(memory_space=pl.ANY)] * len(out_shape)
    if not last:
        out_specs.append(pl.BlockSpec((slots, height), lambda k, *_: (0, 0)))
        out_shape.append(jax.ShapeDtypeStruct((slots, height), jnp.int32))
    flops = 2 * slots * height * tiles * cd_width * columns
    return pl.pallas_call(
        functools.partial(ladder_kernel, len(blocks) > 4 * slots, offsets, start_row, len(earlier), len(chain), stream, pair_rows),
        grid_spec=pltpu.PrefetchScalarGridSpec(
            num_scalar_prefetch=2,
            grid=(cd_width // CHUNK if stream else 1,),
            in_specs=in_specs,
            out_specs=out_specs,
            scratch_shapes=[
                pltpu.VMEM((slots * height, columns), jnp.float32),
                pltpu.VMEM((columns, height), jnp.float32),
                pltpu.VMEM((number, rows, height), jnp.int16),
                pltpu.SemaphoreType.DMA((slots + (number // 2 if last else 1),)),
            ],
        ),
        out_shape=out_shape,
        input_output_aliases=aliases,
        compiler_params=pltpu.CompilerParams(vmem_limit_bytes=STREAM_VMEM if stream else LADDER_VMEM),
        cost_estimate=pl.CostEstimate(flops=flops, bytes_accessed=1 << 20, transcendentals=0),
        name=f"ladder{slots}",
    )(*operands)


def symmetrize_kernel(places, local_rows, pair_rows, mirror, meta, early, late, *refs):
    *pieces, direct, residual, own, rounded, turned, tail, in_sem, out_sem, tail_sem = refs
    core = meta[0]
    moves = []
    for n, piece in enumerate(pieces):
        k, other = n // 2, n % 2
        chips = len(pieces) // 2
        source = (meta[1] + chips - k) % chips * 2 + (1 - core if other else core)
        moves.append(pltpu.make_async_copy(piece.at[core], tail.at[source], tail_sem.at[n]))
        moves[-1].start()
    number, columns = own.shape[0], own.shape[2]
    chips = number // 2
    height = 2 * pair_rows
    depth = local_rows * local_rows
    loads, stores = [], []
    for m in range(number):
        p = mirror[m]
        loads.append(pltpu.make_async_copy(direct.at[p], own.at[m], in_sem.at[m]))
        stores.append(pltpu.make_async_copy(rounded.at[m], residual.at[p], out_sem.at[m]))
        loads[m].start()
    row = lax.broadcasted_iota(jnp.int32, (height, height), 0)
    lane = lax.broadcasted_iota(jnp.int32, (height, height), 1)
    inner = row % pair_rows
    partner = row - inner + (inner % OT) * OT + inner // OT
    pick = jnp.where(lane == partner, 1.0, 0.0).astype(jnp.bfloat16)
    pick = jnp.concatenate([pick, pick], axis=1)
    for move in moves:
        move.wait()
    scales = []
    for i in range(number):
        code = tail[i, depth:, :].astype(jnp.int32).astype(jnp.float32)
        scales.append(jnp.exp2(code) * (1.0 / LEVELS))
    for chip in range(chips):
        for i in range(number):
            place = places(chip, i // 2)
            split = early.shape[1] // depth
            if place < split:
                whole = early[i, place * depth : (place + 1) * depth, :]
            elif place < chips - 1:
                whole = late[i, (place - split) * depth : (place - split + 1) * depth, :]
            else:
                whole = tail[i, :depth, :]
            whole = whole.astype(jnp.int32).astype(jnp.float32)
            whole = whole * scales[i][place : place + 1, :]
            for b in range(local_rows):
                at = (b * number + i) * local_rows
                turned[at : at + local_rows, :] = whole[b * local_rows : (b + 1) * local_rows, :]
        values = turned[...]
        high = values.astype(jnp.bfloat16)
        low = (values - high.astype(jnp.float32)).astype(jnp.bfloat16)
        both = jnp.concatenate([high, low], axis=1)
        mirrored = lax.dot_general(pick, both, (((1,), (1,)), ((), ())), preferred_element_type=jnp.float32)
        for h in range(2):
            m = chip * 2 + h
            loads[m].wait()
            rounded[m] = (own[m] + mirrored[h * pair_rows : (h + 1) * pair_rows, :]).astype(jnp.bfloat16)
            stores[m].start()
    for m in range(number):
        stores[m].wait()


def symmetrize(mirror, meta, early, late, pieces, direct, places):
    number, pair_rows, columns = direct.shape
    local_rows = columns // SPAN
    height = 2 * pair_rows
    return pl.pallas_call(
        functools.partial(symmetrize_kernel, places, local_rows, pair_rows),
        in_specs=[
            pl.BlockSpec(memory_space=pltpu.SMEM),
            pl.BlockSpec(memory_space=pltpu.SMEM),
            pl.BlockSpec(memory_space=pltpu.VMEM),
            pl.BlockSpec(memory_space=pltpu.VMEM),
            *[pl.BlockSpec(memory_space=pl.ANY) for _ in pieces],
            pl.BlockSpec(memory_space=pl.ANY),
        ],
        out_specs=pl.BlockSpec(memory_space=pl.ANY),
        out_shape=jax.ShapeDtypeStruct(direct.shape, jnp.bfloat16),
        scratch_shapes=[
            pltpu.VMEM(direct.shape, jnp.float32),
            pltpu.VMEM(direct.shape, jnp.bfloat16),
            pltpu.VMEM((columns, height), jnp.float32),
            pltpu.VMEM((number, *pieces[0].shape[1:]), jnp.int16),
            pltpu.SemaphoreType.DMA((number,)),
            pltpu.SemaphoreType.DMA((number,)),
            pltpu.SemaphoreType.DMA((number,)),
        ],
        compiler_params=pltpu.CompilerParams(vmem_limit_bytes=SYMMETRIZE_VMEM),
        cost_estimate=pl.CostEstimate(flops=0, bytes_accessed=direct.size * 8, transcendentals=0),
        name="symmetrize",
    )(mirror, meta, early, late, *pieces, hbm(direct))


def local(order, places_of, amps, integrals, domain_mask, tile_list, mirror):
    number = mirror.shape[0]
    pair_rows, cd_width = amps.shape[2:]
    tiles = integrals.shape[0]
    chips = len(order)
    half = chips // 2
    position = [order.index(c) for c in range(chips)]
    me = lax.axis_index("row")
    my_position = jnp.array(position, jnp.int32)[me // 2]
    chip_at = jnp.array(order, jnp.int32)
    core = me % 2

    alive = jnp.take_along_axis(domain_mask, tile_list, axis=1)
    which = jnp.arange(tiles, dtype=jnp.int32)
    hits = (tile_list[:, :, None] == which) * alive[:, :, None]
    wcode = jnp.sum(hits * jnp.arange(1, 3, dtype=jnp.int32)[None, :, None], axis=1).reshape(-1)

    def turn(d):
        return [(order[i] * 2 + c, order[(i + d) % chips] * 2 + c) for i in range(chips) for c in range(2)]

    def shift(x, d, without=()):
        pairs = turn(d)
        return lax.ppermute(x, "row", [p for p in pairs if position[p[1] // 2] not in without])

    def relay(x, targets, d):
        hop = [(order[(r + half + d) % chips], order[r]) for r in targets]
        return lax.ppermute(x, "row", [(a * 2 + c, b * 2 + c) for a, b in hop for c in range(2)])

    def twin(x):
        return lax.ppermute(x, "row", [(i, i ^ 1) for i in range(number)])

    around = chip_at[(my_position + jnp.arange(chips, dtype=jnp.int32)) % chips]
    from_left, from_right = shortcuts(order, places_of)
    skip = sorted(from_left + from_right)
    skips = jnp.array([r in skip for r in range(chips)], jnp.int32)[my_position]
    meta = jnp.concatenate([core[None], around, me[None], skips[None]]).astype(jnp.int32)
    held = load(meta, wcode, integrals)

    left = right = amps
    depth = integrals.shape[2] // number
    split = half // 2 * 2 - 1
    chain, early, codes, order_of = [], [], [], []

    def run(offsets, arrivals, last=False):
        nonlocal chain
        blocks = []
        for a in arrivals:
            blocks += [a, twin(a)] if not last else [*a, *[twin(x) for x in a]]
        if last and skip:
            blocks += [relayed, twin(relayed)]
        offsets = [o % chips for o in offsets]
        if last:
            order_of.extend(offsets)
            return ladder(offsets, meta, wcode, blocks, integrals, True, chain[:1], number, 0, 0, codes)
        late = len(order_of) >= split
        if len(order_of) == split:
            early.append(chain.pop())
        start = (len(order_of) - split if late else len(order_of)) * depth
        rows = (chips - 1 - split if late else split) * depth
        out = ladder(offsets, meta, wcode, blocks, integrals if late else held, late, chain, number, start, rows)
        chain = list(out[:2])
        codes.extend(out[2:])
        order_of.extend(offsets)

    run([0], [amps])
    for s in range(1, half):
        if s > 1:
            left, right, codes[-1] = lax.optimization_barrier((left, right, codes[-1]))
        before = left, right
        left, right = shift(left, 1), shift(right, -1)
        if s == 1:
            nearest = left, right
        if s > 1:
            run([1 - s, s - 1], before)
    if skip:
        relayed = relay(nearest[0], from_left, 1) + relay(nearest[1], from_right, -1)
        left, right, relayed, codes[-1] = lax.optimization_barrier((left, right, relayed, codes[-1]))
    else:
        left, right, codes[-1] = lax.optimization_barrier((left, right, codes[-1]))
    final = shift(left[0, 0], 1, skip), shift(right[0, 1], -1, skip)
    run([1 - half, half - 1], [left, right])
    *final, chain[1] = lax.optimization_barrier((*final, chain[1]))
    direct, *tail = run([half], [final], last=True)
    bulk = [
        lax.all_to_all(m, "row", split_axis=0, concat_axis=0, tiled=True) for m in (early[0], chain[1])
    ]
    pieces = []
    for k in range(chips):
        ahead = [(i, (i + 2 * k) % number) for i in range(number)]
        piece = lax.ppermute(tail[k], "row", ahead) if k else tail[0]
        pieces += [piece, twin(piece)]

    def places(chip, source):
        return order_of.index((position[chip] - position[source]) % chips)

    direct = direct.reshape(number, pair_rows, integrals.shape[2])
    return symmetrize(mirror, meta, *bulk, pieces, direct, places)


def solution(mesh):
    return jax.shard_map(
        functools.partial(local, *ring_order(mesh)),
        mesh=mesh,
        in_specs=(
            P(("groups", "row"), None, None, None),
            P("groups", None, "row"),
            P("groups", None),
            P("groups", None),
            P("groups"),
        ),
        out_specs=P("groups", None, "row"),
        check_vma=False,
    )
```
